32 devices in a mesh: groups: 2 (over y), row: 4 (over z), col: 4 (over x, core).
Axes of the slice: x: 2, y: 2, z: 4, core: 2. Of those that a mesh axis runs over, the one named last changes fastest.
Arguments:
- raw_files: bfloat16 [128, 4, 8, 12000], P(('groups', 'row'), 'col'), parts along dimension 0
- file_channels: int32 [128, 4], P(('groups', 'row'), 'col'), parts along dimension 0, may hold values from 0 to 255, as said below
- reader_counts: int32 [8, 4], P(('groups', 'row'), 'col'), parts along dimension 0, may hold values from 0 to 16, as said below
- fir_taps: float32 [32], replicated, may hold values from -1 to 1
- band_bins: int32 [64], replicated, may hold values from 1 to 1499, as said below
Outputs:
- stack: bfloat16 [512, 4, 64, 128], P(('groups', 'row'), 'col'), parts along dimension 0
The draws below stay inside these ranges and needn't reach their ends.
There are 2 independent parts, one for each index of `groups`. The reference program is written for one: setup_inputs(seed, part) draws one part's arguments, and reference() takes and returns one part's arrays. A program takes and returns all parts, laid end to end along the dimension named above; an argument that names none is the same for every part. Nothing has to cross between parts.
Inputs may be any that keep to these rules, and one draw needn't show every extreme that they name: `file_channels`: channel q belongs to owner row q // 64, column (q // 16) % 4. Every channel stands in exactly one live slot (slot below its reader's count), of a reader in its owner's column. Live slots of one reader name at most 4 channels of one owner; in every column some reader holds exactly 4 channels of every owner. Slots at or above the count hold arbitrary channel numbers. `reader_counts`: in every column some reader holds 16 live slots. `band_bins`: Distinct.
All inputs are finite; a program needn't handle non-finite values.
Results may differ from the reference program's by a relative error of at most 0.017.
Values may be sent and summed in bfloat16 or wider, within the bound.
A program may use at most 64 MiB of HBM per device.

```python
import math
import jax
import jax.numpy as jnp
from jax import lax

CH_DEV = 16
REC = 8
SAMP = 12000
DEC = 4
TAPS = 32
BINS = 64
M = 3000
ROWS = 4
COLS = 4
CAP = 4
SLOTS = 16
FILE_ROWS = 64
CH = 256
COLT = 64


def draw_raw_files(key, part):
    first, second, third = jax.random.split(key, 3)
    shape = (FILE_ROWS, COLS, REC, SAMP)
    scales = jnp.exp(jax.random.uniform(second, (FILE_ROWS, COLS, REC, 1), jnp.float32, 0.0, math.log(10.0)))
    envelope = jnp.exp(jax.random.uniform(third, (SAMP // 8,), jnp.float32, 0.0, math.log(10.0)))
    envelope = jnp.repeat(envelope, 8)
    noise = jax.random.truncated_normal(first, -5.0, 5.0, shape, jnp.float32)
    return (noise * scales * envelope).astype(jnp.bfloat16)


def ingest_plan(key):
    key = jax.random.fold_in(key, 11)
    heavy_key, ticket_key, junk_key, order_key = jax.random.split(key, 4)
    per_column = ROWS * CH_DEV
    heavy = jax.random.randint(heavy_key, (COLS,), 0, ROWS)
    tickets = (ROWS - 1) * CAP
    ticket_keys = jax.random.split(ticket_key, COLS * ROWS)
    picked = jax.vmap(lambda one: jax.random.permutation(one, tickets)[:CH_DEV - CAP])(ticket_keys)
    picked = picked.reshape(COLS, ROWS, CH_DEV - CAP)
    others = picked // CAP
    others = others + (others >= heavy[:, None, None]).astype(jnp.int32)
    heavy_part = jnp.broadcast_to(heavy[:, None, None], (COLS, ROWS, CAP))
    reader_of = jnp.concatenate([heavy_part, others], axis=2).reshape(COLS, per_column).astype(jnp.int32)
    order_keys = jax.random.split(order_key, COLS)
    breaker = jax.vmap(lambda one: jax.random.permutation(one, per_column))(order_keys).astype(jnp.int32)
    ranking = reader_of * per_column + breaker
    order = jnp.argsort(ranking, axis=1, stable=True).astype(jnp.int32)
    counts = jnp.sum((reader_of[:, None, :] == jnp.arange(ROWS, dtype=jnp.int32)[None, :, None]).astype(jnp.int32), axis=2)
    starts = jnp.cumsum(counts, axis=1) - counts
    sorted_reader = jnp.take_along_axis(reader_of, order, axis=1)
    position = jnp.arange(per_column, dtype=jnp.int32)[None, :] - jnp.take_along_axis(starts, sorted_reader, axis=1)
    slot_row = sorted_reader * SLOTS + position
    column_index = jnp.arange(COLS, dtype=jnp.int32)[:, None]
    channel = (order // CH_DEV * COLS + column_index) * CH_DEV + order % CH_DEV
    junk = jax.random.randint(junk_key, (COLS, FILE_ROWS), 0, CH, jnp.int32)
    column_rows = jnp.broadcast_to(column_index, (COLS, per_column))
    lists = junk.at[column_rows, slot_row].set(channel)
    return (lists.T.astype(jnp.int32), counts.T.astype(jnp.int32))


def draw_file_channels(key, part):
    return ingest_plan(key)[0]


def draw_reader_counts(key, part):
    return ingest_plan(key)[1]


def draw_band_bins(key, part):
    key = jax.random.fold_in(key, 5)
    first, second = jax.random.split(key)
    half = M // 2
    inner = (jax.random.permutation(first, half - 3) + 2)[:BINS - 2].astype(jnp.int32)
    every = jnp.concatenate([inner, jnp.array([1, half - 1], jnp.int32)])
    return every[jax.random.permutation(second, BINS)].astype(jnp.int32)


def gaussian(rng, extent, width, limit, kind=jnp.bfloat16):
    return jnp.clip(width * jax.random.normal(rng, extent, jnp.float32), -limit, limit).astype(kind)


def setup_inputs(seed: int = 0, part: int = 0) -> dict:
    streams_of = jax.random.split(jax.random.key(seed), 6)
    own_keys = jax.random.split(jax.random.fold_in(streams_of[5], part), 6)
    return {
        "raw_files": draw_raw_files(jax.random.fold_in(jax.random.fold_in(streams_of[5], part), 71), part),
        "file_channels": draw_file_channels(jax.random.fold_in(jax.random.fold_in(streams_of[5], part), 71), part),
        "reader_counts": draw_reader_counts(jax.random.fold_in(jax.random.fold_in(streams_of[5], part), 71), part),
        "fir_taps": gaussian(streams_of[3], (TAPS,), TAPS ** -0.5, 1.0, jnp.float32),
        "band_bins": draw_band_bins(jax.random.fold_in(streams_of[5], 71), part),
    }


def whiten_block(signal, fir_taps, band_bins):
    count, records, samples = signal.shape
    length = samples // DEC
    widened = jnp.pad(signal.astype(jnp.float32), ((0, 0), (0, 0), (0, TAPS)))
    decimated = jnp.zeros((count, records, length), jnp.float32)
    for offset in range(TAPS):
        decimated = decimated + fir_taps[offset] * widened[:, :, offset:offset + DEC * length:DEC]
    decimated = decimated.astype(jnp.bfloat16)
    steps = jnp.arange(length, dtype=jnp.int32)
    product = band_bins[None, :] * steps[:, None] % length
    angle = 2.0 * math.pi / length * product.astype(jnp.float32)
    table = jnp.concatenate([jnp.cos(angle), -jnp.sin(angle)], axis=1).astype(jnp.bfloat16)
    spectra = jnp.dot(decimated.reshape(count * records, length), table, preferred_element_type=jnp.float32)
    power = lax.optimization_barrier(jnp.mean(spectra * spectra, axis=1, keepdims=True))
    white = spectra / jnp.sqrt(power + 1e-06)
    return white.reshape(count, records, 2 * BINS).astype(jnp.bfloat16)

def reference(raw_files, file_channels, reader_counts, fir_taps, band_bins):
    slot_index = jnp.arange(FILE_ROWS, dtype=jnp.int32)
    within = slot_index % SLOTS
    reader = slot_index // SLOTS
    live = within[:, None] < reader_counts[reader, :]
    target = jnp.where(live, file_channels, CH).astype(jnp.int32)
    signal = jnp.zeros((CH, REC, SAMP), jnp.bfloat16)
    signal = signal.at[target.reshape(-1)].set(raw_files.reshape(FILE_ROWS * COLS, REC, SAMP), mode='drop')
    blocks = signal.reshape(CH // CH_DEV, CH_DEV, REC, SAMP)
    white = lax.map(lambda block: whiten_block(block, fir_taps, band_bins), blocks)
    white = white.reshape(CH, REC, 2 * BINS)
    ordered = white.reshape(ROWS, COLS, CH_DEV, REC, 2 * BINS).transpose(1, 0, 2, 3, 4).reshape(CH, REC, 2 * BINS)
    right = ordered.astype(jnp.float32)
    right_re = right[:, :, :BINS]
    right_im = right[:, :, BINS:]

    def grid_row(block):
        left = block.astype(jnp.float32)
        left_re = left[:, :, :BINS]
        left_im = left[:, :, BINS:]
        real = jnp.einsum('ieb,jeb->ijb', left_re, right_re) + jnp.einsum('ieb,jeb->ijb', left_im, right_im)
        imag = jnp.einsum('ieb,jeb->ijb', left_im, right_re) - jnp.einsum('ieb,jeb->ijb', left_re, right_im)
        joined = jnp.concatenate([real, imag], axis=2) / REC
        return joined.astype(jnp.bfloat16)
    rows_of_grid = white.reshape(ROWS, COLS * CH_DEV, REC, 2 * BINS)
    result = lax.map(grid_row, rows_of_grid)
    return result.reshape(CH, COLS, COLT, 2 * BINS)
```

```python
import functools
import math

import jax
import jax.numpy as jnp
from jax import lax
from jax.experimental import pallas as pl
from jax.experimental.pallas import tpu as pltpu
from jax.sharding import PartitionSpec as P

CH_DEV = 16
DEC = 4
LANES = 128
SPAN = 512
PIECE = 2048
MESH = pl.DeviceIdType.MESH
F32 = jnp.float32
BF16 = jnp.bfloat16


def turn_cos(steps, period):
    rest = steps - period * jnp.floor(steps * (1.0 / period) + 0.5)
    y = (period / 4.0 - jnp.abs(rest)) * (2.0 * math.pi / period)
    z = y * y
    poly = -1.0 / 39916800.0
    for factor in (1.0 / 362880.0, -1.0 / 5040.0, 1.0 / 120.0, -1.0 / 6.0, 1.0):
        poly = poly * z + factor
    return poly * y


def gather_kernel(
    nrows, ncols, slots, records, samples, taps,
    x_hbm, chan_ref, count_ref, fir_ref, bins_ref,
    right_ref, left_ref,
    x_ref, table_ref, edge_ref, cos_ref, sin_ref, white_ref, col_ref, label_ref,
    load_sem, lsend, lrecv, rsend, rrecv, csend, crecv,
):
    me_row = lax.axis_index("row")
    me_col = lax.axis_index("col")
    barrier = pltpu.get_barrier_semaphore()
    for d in range(1, nrows):
        pl.semaphore_signal(barrier, inc=1, device_id={"row": lax.rem(me_row + d, nrows)}, device_id_type=MESH)
    for d in range(1, ncols):
        pl.semaphore_signal(barrier, inc=1, device_id={"col": lax.rem(me_col + d, ncols)}, device_id_type=MESH)

    pieces = [(s, min(PIECE, samples - s)) for s in range(0, samples, PIECE)]
    loads = []
    for n, (start, size) in enumerate(pieces):
        load = pltpu.make_async_copy(
            x_hbm.at[:, pl.ds(start, size)], x_ref.at[:, pl.ds(start, size)], load_sem.at[n]
        )
        load.start()
        loads.append(load)

    width = nrows * slots
    count = count_ref[0]
    lane = lax.broadcasted_iota(jnp.int32, (8, width), 1)
    label = jnp.full((8, width), -1, jnp.int32)
    for s in range(slots):
        channel = jnp.where(s < count, chan_ref[s], -1)
        label = jnp.where(lane == me_row * slots + s, channel, label)
    label_ref[me_row] = label

    pl.semaphore_wait(barrier, nrows - 1 + ncols - 1)
    label_copies = []
    for d in range(1, nrows):
        copy = pltpu.make_async_remote_copy(
            src_ref=label_ref.at[me_row], dst_ref=label_ref.at[me_row],
            send_sem=lsend.at[d], recv_sem=lrecv.at[d],
            device_id={"row": lax.rem(me_row + d, nrows)}, device_id_type=MESH,
        )
        copy.start()
        label_copies.append(copy)

    length = samples // DEC
    half = LANES // 2
    lane8 = lax.broadcasted_iota(jnp.int32, (8, LANES), 1)
    sub8 = lax.broadcasted_iota(jnp.int32, (8, LANES), 0)
    upper = lane8 >= half
    binlane = jnp.where(upper, lane8 - half, lane8)
    bins = jnp.zeros((8, LANES), jnp.int32)
    for k in range(half):
        bins = jnp.where(binlane == k, bins_ref[k], bins)
    bins = bins.astype(F32)
    quarter = length / 4.0
    off1 = jnp.where(upper, quarter, 0.0)
    off2 = jnp.where(upper, 2.0 * quarter, quarter)
    phase = sub8 % DEC
    later = sub8 // DEC
    groups = taps // DEC
    filt = []
    for i in range(groups):
        f = jnp.zeros((8, LANES), F32)
        for p in range(DEC):
            f = jnp.where(phase == p, fir_ref[DEC * i + p], f)
        filt.append(f)
    base1 = jnp.zeros((8, LANES), F32)
    base2 = jnp.zeros((8, LANES), F32)
    for i in range(groups):
        steps = bins * (later - i).astype(F32)
        base1 = base1 + filt[i] * turn_cos(steps + off1, length)
        base2 = base2 + filt[i] * turn_cos(steps + off2, length)
    turns = SPAN // 8
    hops = pl.cdiv(samples, SPAN)
    hop_rows = pl.cdiv(hops, 8) * 8
    for a in range(0, turns, 8):
        steps = bins * ((sub8 + a) * (8 // DEC)).astype(F32)
        cos_ref[pl.ds(a, 8), :] = turn_cos(steps, length)
        sin_ref[pl.ds(a, 8), :] = turn_cos(steps - quarter, length)
    for a in range(0, hop_rows, 8):
        steps = bins * ((sub8 + a) * (SPAN // DEC)).astype(F32)
        cos_ref[pl.ds(turns + a, 8), :] = turn_cos(steps, length)
        sin_ref[pl.ds(turns + a, 8), :] = turn_cos(steps - quarter, length)
    for a in range(0, turns, 2):
        one, two = [], []
        for b in (a, a + 1):
            c = cos_ref[pl.ds(b, 1), :]
            s = sin_ref[pl.ds(b, 1), :]
            one.append(c * base1 + s * base2)
            two.append(c * base2 - s * base1)
        table_ref[pl.ds(8 * a, 16), pl.ds(0, LANES)] = jnp.concatenate(one, axis=0).astype(BF16)
        table_ref[pl.ds(8 * a, 16), pl.ds(LANES, LANES)] = jnp.concatenate(two, axis=0).astype(BF16)
    per = 8 // DEC
    edge_ref[...] = jnp.zeros(edge_ref.shape, BF16)
    before = {}
    for dist in range(-(groups - 1), 0):
        n = later + dist
        before[dist] = jnp.where(n < 0, turn_cos(bins * n.astype(F32) + off1, length), 0.0)
    edges = pl.cdiv(taps, 16) * 2
    rows = []
    for a in range(edges):
        fix = jnp.zeros((8, LANES), F32)
        for i in range(groups):
            if per * a - i < 0:
                fix = fix - filt[i] * before[per * a - i]
        rows.append(fix)
    for a in range(0, edges, 2):
        edge_ref[pl.ds(8 * a, 16), :] = jnp.concatenate(rows[a:a + 2], axis=0).astype(BF16)

    count_rows = slots * records
    total = jnp.zeros((count_rows, LANES), F32)
    ready = 0
    for h in range(hops):
        start = h * SPAN
        size = min(SPAN, samples - start)
        while ready < len(pieces) and pieces[ready][0] < start + size:
            loads[ready].wait()
            ready += 1
        part = jnp.dot(x_ref[:, pl.ds(start, size)], table_ref[pl.ds(0, size), :], preferred_element_type=F32)
        c = cos_ref[pl.ds(turns + h, 1), :]
        s = sin_ref[pl.ds(turns + h, 1), :]
        total = total + part[:, :LANES] * c + part[:, LANES:] * s
    total = total + jnp.dot(x_ref[:, pl.ds(0, LANES)], edge_ref[...], preferred_element_type=F32)
    power = jnp.mean(total * total, axis=1, keepdims=True)
    white_ref[...] = total * lax.rsqrt(power + 1e-06)
    alive = lax.broadcasted_iota(jnp.int32, (slots, LANES), 0) < count
    for e in range(records):
        rows = white_ref[pl.ds(e, slots, stride=records), :]
        col_ref[me_row, e] = jnp.where(alive, rows, 0.0).astype(BF16)

    row_copies = []
    for d in range(1, nrows):
        copy = pltpu.make_async_remote_copy(
            src_ref=col_ref.at[me_row], dst_ref=col_ref.at[me_row],
            send_sem=rsend.at[d], recv_sem=rrecv.at[d],
            device_id={"row": lax.rem(me_row + d, nrows)}, device_id_type=MESH,
        )
        copy.start()
        row_copies.append(copy)
    for copy in label_copies:
        copy.wait()
    label = label_ref[0]
    for r in range(1, nrows):
        label = jnp.maximum(label, label_ref[r])
    channels = nrows * CH_DEV
    order = lax.broadcasted_iota(jnp.int32, (channels, width), 0)
    wanted = (order // CH_DEV) * (ncols * CH_DEV) + me_col * CH_DEV + order % CH_DEV
    pick = (wanted == label[0:1, :]).astype(F32).astype(BF16)
    for copy in row_copies:
        copy.wait()
    for e in range(records):
        rows = jnp.concatenate([col_ref[r, e] for r in range(nrows)], axis=0)
        right_ref[e] = jnp.dot(pick, rows, preferred_element_type=F32).astype(BF16)
    first = pl.multiple_of(me_row * CH_DEV, CH_DEV)
    for e in range(records):
        left_ref[me_col, e] = right_ref[e, pl.ds(first, CH_DEV), :]
    col_copies = []
    for d in range(1, ncols):
        copy = pltpu.make_async_remote_copy(
            src_ref=left_ref.at[me_col], dst_ref=left_ref.at[me_col],
            send_sem=csend.at[d], recv_sem=crecv.at[d],
            device_id={"col": lax.rem(me_col + d, ncols)}, device_id_type=MESH,
        )
        copy.start()
        col_copies.append(copy)
    for copy in col_copies:
        copy.wait()


def pair_kernel(records, left_ref, right_ref, out_ref, u1_ref, u2_ref, v1_ref, v2_ref):
    half = LANES // 2
    channels = right_ref.shape[1]

    @pl.when(pl.program_id(0) == 0)
    def _():
        upper = lax.broadcasted_iota(jnp.int32, (channels, LANES), 1) >= half
        for e in range(records):
            v = right_ref[e].astype(F32)
            w = pltpu.roll(v, half, 1)
            v1_ref[e] = jnp.where(upper, w, v)
            v2_ref[e] = jnp.where(upper, v, w)

    upper = lax.broadcasted_iota(jnp.int32, (CH_DEV, LANES), 1) >= half
    scale = 1.0 / records
    for e in range(records):
        u = left_ref[0, e].astype(F32) * scale
        w = pltpu.roll(u, half, 1)
        u1_ref[e] = u
        u2_ref[e] = jnp.where(upper, -w, w)

    @pl.loop(0, channels // 16)
    def _(jb):
        at = pl.ds(pl.multiple_of(jb * 16, 16), 16)
        v1 = [v1_ref[e, at, :] for e in range(records)]
        v2 = [v2_ref[e, at, :] for e in range(records)]
        for i in range(CH_DEV):
            total = u1_ref[0, pl.ds(i, 1), :] * v1[0] + u2_ref[0, pl.ds(i, 1), :] * v2[0]
            for e in range(1, records):
                total = total + u1_ref[e, pl.ds(i, 1), :] * v1[e]
                total = total + u2_ref[e, pl.ds(i, 1), :] * v2[e]
            out_ref[i, at, :] = total.astype(BF16)


def on_device(raw_files, file_channels, reader_counts, fir_taps, band_bins):
    nrows = lax.axis_size("row")
    ncols = lax.axis_size("col")
    slots, _, records, samples = raw_files.shape
    taps = fir_taps.shape[0]
    width = nrows * slots
    channels = nrows * CH_DEV
    signal = raw_files.reshape(slots * records, samples)
    hop_rows = pl.cdiv(pl.cdiv(samples, SPAN), 8) * 8
    tall = SPAN // 8 + hop_rows
    smem = pl.BlockSpec(memory_space=pltpu.SMEM)
    vmem = pl.BlockSpec(memory_space=pltpu.VMEM)
    right, left = pl.pallas_call(
        functools.partial(gather_kernel, nrows, ncols, slots, records, samples, taps),
        out_shape=(
            jax.ShapeDtypeStruct((records, channels, LANES), BF16),
            jax.ShapeDtypeStruct((ncols, records, CH_DEV, LANES), BF16),
        ),
        in_specs=[pl.BlockSpec(memory_space=pl.ANY), smem, smem, smem, smem],
        out_specs=(vmem, vmem),
        scratch_shapes=[
            pltpu.VMEM((slots * records, samples), BF16),
            pltpu.VMEM((SPAN, 2 * LANES), BF16),
            pltpu.VMEM((LANES, LANES), BF16),
            pltpu.VMEM((tall, LANES), F32),
            pltpu.VMEM((tall, LANES), F32),
            pltpu.VMEM((slots * records, LANES), F32),
            pltpu.VMEM((nrows, records, slots, LANES), BF16),
            pltpu.VMEM((nrows, 8, width), jnp.int32),
            pltpu.SemaphoreType.DMA((pl.cdiv(samples, PIECE),)),
            pltpu.SemaphoreType.DMA((nrows,)),
            pltpu.SemaphoreType.DMA((nrows,)),
            pltpu.SemaphoreType.DMA((nrows,)),
            pltpu.SemaphoreType.DMA((nrows,)),
            pltpu.SemaphoreType.DMA((ncols,)),
            pltpu.SemaphoreType.DMA((ncols,)),
        ],
        compiler_params=pltpu.CompilerParams(
            collective_id=0, has_side_effects=True, vmem_limit_bytes=40 * 2**20
        ),
    )(signal, file_channels.reshape(-1), reader_counts.reshape(-1), fir_taps, band_bins)
    stacked = pl.pallas_call(
        functools.partial(pair_kernel, records),
        grid=(ncols,),
        out_shape=jax.ShapeDtypeStruct((ncols * CH_DEV, channels, LANES), BF16),
        in_specs=[
            pl.BlockSpec((1, records, CH_DEV, LANES), lambda c: (c, 0, 0, 0)),
            pl.BlockSpec((records, channels, LANES), lambda c: (0, 0, 0)),
        ],
        out_specs=pl.BlockSpec((CH_DEV, channels, LANES), lambda c: (c, 0, 0)),
        scratch_shapes=[
            pltpu.VMEM((records, CH_DEV, LANES), F32),
            pltpu.VMEM((records, CH_DEV, LANES), F32),
            pltpu.VMEM((records, channels, LANES), F32),
            pltpu.VMEM((records, channels, LANES), F32),
        ],
        compiler_params=pltpu.CompilerParams(vmem_limit_bytes=40 * 2**20),
    )(left, right)
    return stacked[:, None, :, :]


def solution(mesh):
    return jax.shard_map(
        on_device,
        mesh=mesh,
        in_specs=(
            P(("groups", "row"), "col", None, None),
            P(("groups", "row"), "col"),
            P(("groups", "row"), "col"),
            P(),
            P(),
        ),
        out_specs=P(("groups", "row"), "col", None, None),
        check_vma=False,
    )
```

```python
import functools
import math

import jax
import jax.numpy as jnp
from jax import lax
from jax.experimental import pallas as pl
from jax.experimental.pallas import tpu as pltpu
from jax.sharding import PartitionSpec as P

CH_DEV = 16
DEC = 4
LANES = 128
SPAN = 512
PIECE = 2048
MESH = pl.DeviceIdType.MESH
F32 = jnp.float32
BF16 = jnp.bfloat16


def turn_cos(steps, period):
    rest = steps - period * jnp.floor(steps * (1.0 / period) + 0.5)
    y = (period / 4.0 - jnp.abs(rest)) * (2.0 * math.pi / period)
    z = y * y
    poly = -1.0 / 39916800.0
    for factor in (1.0 / 362880.0, -1.0 / 5040.0, 1.0 / 120.0, -1.0 / 6.0, 1.0):
        poly = poly * z + factor
    return poly * y


def gather_kernel(
    nrows, ncols, slots, records, samples, taps,
    x_hbm, chan_hbm, count_hbm, fir_hbm, bins_hbm,
    out_hbm,
    chan_ref, count_ref, fir_ref, bins_ref, x_ref, table_ref, edge_ref, cos_ref, sin_ref, white_ref, col_ref, label_ref,
    left_ref, u1_ref, u2_ref, v1_ref, v2_ref, block_ref,
    store_sem, load_sem, small_sem, lsend, lrecv, rsend, rrecv, csend, crecv,
):
    me_row = lax.axis_index("row")
    me_col = lax.axis_index("col")
    barrier = pltpu.get_barrier_semaphore()
    for d in range(1, nrows):
        pl.semaphore_signal(barrier, inc=1, device_id={"row": lax.rem(me_row + d, nrows)}, device_id_type=MESH)
    for d in range(1, ncols):
        pl.semaphore_signal(barrier, inc=1, device_id={"col": lax.rem(me_col + d, ncols)}, device_id_type=MESH)

    small = []
    for n, (src, dst) in enumerate(
        ((chan_hbm, chan_ref), (count_hbm, count_ref), (fir_hbm, fir_ref), (bins_hbm, bins_ref))
    ):
        small.append(pltpu.make_async_copy(src, dst, small_sem.at[n]))
        small[-1].start()
    pieces = [(s, min(PIECE, samples - s)) for s in range(0, samples, PIECE)]
    loads = []
    for n, (start, size) in enumerate(pieces):
        load = pltpu.make_async_copy(
            x_hbm.at[:, pl.ds(start, size)], x_ref.at[:, pl.ds(start, size)], load_sem.at[n]
        )
        load.start()
        loads.append(load)

    width = nrows * slots
    for copy in small:
        copy.wait()
    count = count_ref[0]
    lane = lax.broadcasted_iota(jnp.int32, (8, width), 1)
    label = jnp.full((8, width), -1, jnp.int32)
    for s in range(slots):
        channel = jnp.where(s < count, chan_ref[s], -1)
        label = jnp.where(lane == me_row * slots + s, channel, label)
    label_ref[me_row] = label

    pl.semaphore_wait(barrier, nrows - 1 + ncols - 1)
    label_copies = []
    for d in range(1, nrows):
        copy = pltpu.make_async_remote_copy(
            src_ref=label_ref.at[me_row], dst_ref=label_ref.at[me_row],
            send_sem=lsend.at[d], recv_sem=lrecv.at[d],
            device_id={"row": lax.rem(me_row + d, nrows)}, device_id_type=MESH,
        )
        copy.start()
        label_copies.append(copy)

    length = samples // DEC
    half = LANES // 2
    lane8 = lax.broadcasted_iota(jnp.int32, (8, LANES), 1)
    sub8 = lax.broadcasted_iota(jnp.int32, (8, LANES), 0)
    upper = lane8 >= half
    binlane = jnp.where(upper, lane8 - half, lane8)
    bins = jnp.zeros((8, LANES), jnp.int32)
    for k in range(half):
        bins = jnp.where(binlane == k, bins_ref[k], bins)
    bins = bins.astype(F32)
    quarter = length / 4.0
    off1 = jnp.where(upper, quarter, 0.0)
    off2 = jnp.where(upper, 2.0 * quarter, quarter)
    phase = sub8 % DEC
    later = sub8 // DEC
    groups = taps // DEC
    filt = []
    for i in range(groups):
        f = jnp.zeros((8, LANES), F32)
        for p in range(DEC):
            f = jnp.where(phase == p, fir_ref[DEC * i + p], f)
        filt.append(f)
    base1 = jnp.zeros((8, LANES), F32)
    base2 = jnp.zeros((8, LANES), F32)
    for i in range(groups):
        steps = bins * (later - i).astype(F32)
        base1 = base1 + filt[i] * turn_cos(steps + off1, length)
        base2 = base2 + filt[i] * turn_cos(steps + off2, length)
    turns = SPAN // 8
    hops = pl.cdiv(samples, SPAN)
    hop_rows = pl.cdiv(hops, 8) * 8
    for a in range(0, turns, 8):
        steps = bins * ((sub8 + a) * (8 // DEC)).astype(F32)
        cos_ref[pl.ds(a, 8), :] = turn_cos(steps, length)
        sin_ref[pl.ds(a, 8), :] = turn_cos(steps - quarter, length)
    for a in range(0, hop_rows, 8):
        steps = bins * ((sub8 + a) * (SPAN // DEC)).astype(F32)
        cos_ref[pl.ds(turns + a, 8), :] = turn_cos(steps, length)
        sin_ref[pl.ds(turns + a, 8), :] = turn_cos(steps - quarter, length)
    for a in range(0, turns, 2):
        one, two = [], []
        for b in (a, a + 1):
            c = cos_ref[pl.ds(b, 1), :]
            s = sin_ref[pl.ds(b, 1), :]
            one.append(c * base1 + s * base2)
            two.append(c * base2 - s * base1)
        table_ref[pl.ds(8 * a, 16), pl.ds(0, LANES)] = jnp.concatenate(one, axis=0).astype(BF16)
        table_ref[pl.ds(8 * a, 16), pl.ds(LANES, LANES)] = jnp.concatenate(two, axis=0).astype(BF16)
    per = 8 // DEC
    edge_ref[...] = jnp.zeros(edge_ref.shape, BF16)
    before = {}
    for dist in range(-(groups - 1), 0):
        n = later + dist
        before[dist] = jnp.where(n < 0, turn_cos(bins * n.astype(F32) + off1, length), 0.0)
    edges = pl.cdiv(taps, 16) * 2
    rows = []
    for a in range(edges):
        fix = jnp.zeros((8, LANES), F32)
        for i in range(groups):
            if per * a - i < 0:
                fix = fix - filt[i] * before[per * a - i]
        rows.append(fix)
    for a in range(0, edges, 2):
        edge_ref[pl.ds(8 * a, 16), :] = jnp.concatenate(rows[a:a + 2], axis=0).astype(BF16)

    count_rows = slots * records
    total = jnp.zeros((count_rows, LANES), F32)
    ready = 0
    for h in range(hops):
        start = h * SPAN
        size = min(SPAN, samples - start)
        while ready < len(pieces) and pieces[ready][0] < start + size:
            loads[ready].wait()
            ready += 1
        part = jnp.dot(x_ref[:, pl.ds(start, size)], table_ref[pl.ds(0, size), :], preferred_element_type=F32)
        c = cos_ref[pl.ds(turns + h, 1), :]
        s = sin_ref[pl.ds(turns + h, 1), :]
        total = total + part[:, :LANES] * c + part[:, LANES:] * s
    total = total + jnp.dot(x_ref[:, pl.ds(0, LANES)], edge_ref[...], preferred_element_type=F32)
    power = jnp.mean(total * total, axis=1, keepdims=True)
    white_ref[...] = total * lax.rsqrt(power + 1e-06)
    alive = lax.broadcasted_iota(jnp.int32, (slots, LANES), 0) < count
    for e in range(records):
        rows = white_ref[pl.ds(e, slots, stride=records), :]
        col_ref[me_row, e] = jnp.where(alive, rows, 0.0).astype(BF16)

    row_copies = []
    for d in range(1, nrows):
        copy = pltpu.make_async_remote_copy(
            src_ref=col_ref.at[me_row], dst_ref=col_ref.at[me_row],
            send_sem=rsend.at[d], recv_sem=rrecv.at[d],
            device_id={"row": lax.rem(me_row + d, nrows)}, device_id_type=MESH,
        )
        copy.start()
        row_copies.append(copy)
    for copy in label_copies:
        copy.wait()
    label = label_ref[0]
    for r in range(1, nrows):
        label = jnp.maximum(label, label_ref[r])
    channels = nrows * CH_DEV
    order = lax.broadcasted_iota(jnp.int32, (channels, width), 0)
    wanted = (order // CH_DEV) * (ncols * CH_DEV) + me_col * CH_DEV + order % CH_DEV
    pick = (wanted == label[0:1, :]).astype(F32).astype(BF16)
    for copy in row_copies:
        copy.wait()
    wide = lax.broadcasted_iota(jnp.int32, (channels, LANES), 1) >= half
    for e in range(records):
        rows = jnp.concatenate([col_ref[r, e] for r in range(nrows)], axis=0)
        v = jnp.dot(pick, rows, preferred_element_type=F32)
        w = pltpu.roll(v, half, 1)
        v1_ref[e] = jnp.where(wide, w, v)
        v2_ref[e] = jnp.where(wide, v, w)
    first = pl.multiple_of(me_row * CH_DEV, CH_DEV)
    own = lax.broadcasted_iota(jnp.int32, (CH_DEV, LANES), 1) >= half
    for e in range(records):
        v1 = v1_ref[e, pl.ds(first, CH_DEV), :]
        v2 = v2_ref[e, pl.ds(first, CH_DEV), :]
        left_ref[me_col, e] = jnp.where(own, v2, v1).astype(BF16)
    col_copies = []
    for d in range(1, ncols):
        copy = pltpu.make_async_remote_copy(
            src_ref=left_ref.at[me_col], dst_ref=left_ref.at[me_col],
            send_sem=csend.at[d], recv_sem=crecv.at[d],
            device_id={"col": lax.rem(me_col + d, ncols)}, device_id_type=MESH,
        )
        copy.start()
        col_copies.append(copy)
    scale = 1.0 / records
    stores = []
    for d in range(ncols):
        source = lax.rem(me_col + ncols - d, ncols)
        if d > 0:
            pltpu.make_async_remote_copy(
                src_ref=left_ref.at[source], dst_ref=left_ref.at[source],
                send_sem=csend.at[d], recv_sem=crecv.at[d],
                device_id={"col": source}, device_id_type=MESH,
            ).wait_recv()
        for e in range(records):
            u = left_ref[source, e].astype(F32) * scale
            w = pltpu.roll(u, half, 1)
            u1_ref[e] = u
            u2_ref[e] = jnp.where(own, -w, w)

        @pl.loop(0, channels // 16)
        def _(jb):
            at = pl.ds(pl.multiple_of(jb * 16, 16), 16)
            v1 = [v1_ref[e, at, :] for e in range(records)]
            v2 = [v2_ref[e, at, :] for e in range(records)]
            for i in range(CH_DEV):
                total = u1_ref[0, pl.ds(i, 1), :] * v1[0] + u2_ref[0, pl.ds(i, 1), :] * v2[0]
                for e in range(1, records):
                    total = total + u1_ref[e, pl.ds(i, 1), :] * v1[e]
                    total = total + u2_ref[e, pl.ds(i, 1), :] * v2[e]
                block_ref[source, i, at, :] = total.astype(BF16)

        store = pltpu.make_async_copy(block_ref.at[source], out_hbm.at[source], store_sem.at[d])
        store.start()
        stores.append(store)
    for copy in col_copies:
        copy.wait_send()
    for store in stores:
        store.wait()


def on_device(raw_files, file_channels, reader_counts, fir_taps, band_bins):
    nrows = lax.axis_size("row")
    ncols = lax.axis_size("col")
    slots, _, records, samples = raw_files.shape
    taps = fir_taps.shape[0]
    width = nrows * slots
    channels = nrows * CH_DEV
    signal = raw_files.reshape(slots * records, samples)
    hop_rows = pl.cdiv(pl.cdiv(samples, SPAN), 8) * 8
    tall = SPAN // 8 + hop_rows
    stacked = pl.pallas_call(
        functools.partial(gather_kernel, nrows, ncols, slots, records, samples, taps),
        out_shape=jax.ShapeDtypeStruct((ncols, CH_DEV, channels, LANES), BF16),
        in_specs=[pl.BlockSpec(memory_space=pltpu.HBM)] * 5,
        out_specs=pl.BlockSpec(memory_space=pltpu.HBM),
        scratch_shapes=[
            pltpu.SMEM((slots,), jnp.int32),
            pltpu.SMEM((1,), jnp.int32),
            pltpu.SMEM(fir_taps.shape, F32),
            pltpu.SMEM(band_bins.shape, jnp.int32),
            pltpu.VMEM((slots * records, samples), BF16),
            pltpu.VMEM((SPAN, 2 * LANES), BF16),
            pltpu.VMEM((LANES, LANES), BF16),
            pltpu.VMEM((tall, LANES), F32),
            pltpu.VMEM((tall, LANES), F32),
            pltpu.VMEM((slots * records, LANES), F32),
            pltpu.VMEM((nrows, records, slots, LANES), BF16),
            pltpu.VMEM((nrows, 8, width), jnp.int32),
            pltpu.VMEM((ncols, records, CH_DEV, LANES), BF16),
            pltpu.VMEM((records, CH_DEV, LANES), F32),
            pltpu.VMEM((records, CH_DEV, LANES), F32),
            pltpu.VMEM((records, channels, LANES), F32),
            pltpu.VMEM((records, channels, LANES), F32),
            pltpu.VMEM((ncols, CH_DEV, channels, LANES), BF16),
            pltpu.SemaphoreType.DMA((ncols,)),
            pltpu.SemaphoreType.DMA((pl.cdiv(samples, PIECE),)),
            pltpu.SemaphoreType.DMA((4,)),
            pltpu.SemaphoreType.DMA((nrows,)),
            pltpu.SemaphoreType.DMA((nrows,)),
            pltpu.SemaphoreType.DMA((nrows,)),
            pltpu.SemaphoreType.DMA((nrows,)),
            pltpu.SemaphoreType.DMA((ncols,)),
            pltpu.SemaphoreType.DMA((ncols,)),
        ],
        compiler_params=pltpu.CompilerParams(
            collective_id=0, has_side_effects=True, vmem_limit_bytes=60 * 2**20
        ),
    )(signal, file_channels.reshape(-1), reader_counts.reshape(-1), fir_taps, band_bins)
    return stacked.reshape(ncols * CH_DEV, 1, channels, LANES)


def solution(mesh):
    return jax.shard_map(
        on_device,
        mesh=mesh,
        in_specs=(
            P(("groups", "row"), "col", None, None),
            P(("groups", "row"), "col"),
            P(("groups", "row"), "col"),
            P(),
            P(),
        ),
        out_specs=P(("groups", "row"), "col", None, None),
        check_vma=False,
    )
```
